1024 devices in a mesh: dp: 512 (over y_lo, x, z, core), sub: 2 (over y_hi).
Axes of the slice: x: 8, y: 8 (y_hi: 2, y_lo: 4; y = y_hi * 4 + y_lo), z: 8, core: 2. Of those that a mesh axis runs over, the one named last changes fastest.
Arguments:
- picture_encoder_embeds: float32 [131072, 1152], P(('dp', 'sub')), may hold values from -0.24 to 0.24
- caption_encoder_embeds: float32 [131072, 1152], P(('dp', 'sub')), may hold values from -0.24 to 0.24
- score_multiplier: float32 [], replicated, may hold values from 2 to 10
- score_offset_term: float32 [], replicated, may hold values from -4 to -1
Outputs:
- image_grad: float32 [131072, 1152], P(('dp', 'sub'))
- text_grad: float32 [131072, 1152], P(('dp', 'sub'))
The draws below stay inside these ranges and needn't reach their ends.
All inputs are finite; a program needn't handle non-finite values.
Results may differ from the reference program's by a relative error of at most 0.005.
Values may be sent and summed in bfloat16 or wider, within the bound.
No kernel may reach another device: no remote copies, remote signals or barrier semaphores. Data moves between devices by JAX's collectives and lax.ppermute only.
A program may use at most 32 MiB of HBM per device.

```python
import math
import jax
import jax.numpy as jnp
from jax import lax

D = 1152
GROUP = 256
BLOCKS = 512
PAIRS = 131072


def levels(rng, shape, cuts, smallest, top_value):
    gain = 1.0
    for dim, blocks in cuts:
        steps = jax.random.uniform(jax.random.fold_in(jax.random.fold_in(rng, 6), dim), (blocks,), jnp.float32, smallest / len(cuts), top_value / len(cuts))
        gain = gain * jnp.repeat(jnp.exp(steps), shape[dim] // blocks).reshape((-1,) + (1,) * (len(shape) - 1 - dim))
    return gain


def noise(rng, shape, deviation, most, cuts=(), kind=jnp.bfloat16):
    result = deviation * jax.random.normal(rng, shape, jnp.float32)
    if cuts:
        result = result * levels(rng, shape, cuts, -0.22, 0.18)
    return jnp.clip(result, -most, most).astype(kind)


def setup_inputs(seed: int = 0) -> dict:
    arg_keys = jax.random.split(jax.random.key(seed), 5)
    return {
        "picture_encoder_embeds": noise(arg_keys[0], (PAIRS, D), 0.03, 0.24, ((0, 1024),), jnp.float32),
        "caption_encoder_embeds": noise(arg_keys[1], (PAIRS, D), 0.03, 0.24, ((0, 1024),), jnp.float32),
        "score_multiplier": jnp.clip(jnp.exp(jax.random.uniform(arg_keys[2], (), jnp.float32, math.log(2.0), math.log(10.0))), 2.0, 10.0),
        "score_offset_term": jnp.clip(jax.random.uniform(arg_keys[3], (), jnp.float32, -4.0, -1.0), -4.0, -1.0),
    }


def normalize(values):
    inverse = lax.rsqrt(lax.optimization_barrier(jnp.sum(values * values, axis=-1, keepdims=True)) + 1e-06)
    return (values * inverse, inverse)

def backward_norm(unit, inverse, direction):
    return (direction - unit * lax.optimization_barrier(jnp.sum(unit * direction, axis=-1, keepdims=True))) * inverse

def reference(picture_encoder_embeds, caption_encoder_embeds, score_multiplier, score_offset_term):
    image_unit, image_inverse = normalize(picture_encoder_embeds)
    text_unit, text_inverse = normalize(caption_encoder_embeds)
    picture_first_index = image_unit.astype(jnp.bfloat16)
    text_low = text_unit.astype(jnp.bfloat16)
    text_groups = text_low.reshape(BLOCKS, GROUP, D)
    window = jnp.concatenate([jnp.roll(text_groups, 1, axis=0), text_groups, jnp.roll(text_groups, -1, axis=0)], axis=1)
    image_groups = picture_first_index.reshape(BLOCKS, GROUP, D)
    row_ids = lax.broadcasted_iota(jnp.int32, (GROUP, 3 * GROUP), 0)
    col_ids = lax.broadcasted_iota(jnp.int32, (GROUP, 3 * GROUP), 1)
    match_sign_label = jnp.where(col_ids == row_ids + GROUP, jnp.float32(1.0), jnp.float32(-1.0))

    def per_block(block_args):
        earlier_entries, later_entries = block_args
        similarity_scores = score_multiplier * jnp.dot(earlier_entries, later_entries.T, preferred_element_type=jnp.float32) + score_offset_term
        derivative_weights = (-match_sign_label * score_multiplier * jax.nn.sigmoid(-match_sign_label * similarity_scores)).astype(jnp.bfloat16)
        image_part = jnp.dot(derivative_weights, later_entries, preferred_element_type=jnp.float32)
        window_part = jnp.dot(derivative_weights.T, earlier_entries, preferred_element_type=jnp.float32)
        return (image_part, window_part)
    image_dir, window_dir = lax.map(per_block, (image_groups, window))
    window_dir = window_dir.reshape(BLOCKS, 3, GROUP, D)
    text_dir = window_dir[:, 1] + jnp.roll(window_dir[:, 0], -1, axis=0) + jnp.roll(window_dir[:, 2], 1, axis=0)
    image_grad = backward_norm(image_unit, image_inverse, image_dir.reshape(PAIRS, D))
    text_grad = backward_norm(text_unit, text_inverse, text_dir.reshape(PAIRS, D))
    return (image_grad, text_grad)
```

```python
import jax
import jax.numpy as jnp
from jax import lax
from jax.experimental import pallas as pl
from jax.experimental.pallas import tpu as pltpu
from jax.sharding import PartitionSpec as P

BF16 = jnp.bfloat16
F32 = jnp.float32
VMEM = pl.BlockSpec(memory_space=pltpu.VMEM)
SMEM = pl.BlockSpec(memory_space=pltpu.SMEM)


def times_transposed(a, b):
    return lax.dot_general(a, b, (((1,), (1,)), ((), ())), preferred_element_type=F32)


def times(a, b):
    return lax.dot_general(a, b, (((1,), (0,)), ((), ())), preferred_element_type=F32)


def inverse_norm(values):
    return lax.rsqrt(jnp.sum(values * values, axis=-1, keepdims=True) + 1e-06)


def backward_norm(values, direction):
    inverse = inverse_norm(values)
    unit = values * inverse
    return (direction - unit * jnp.sum(unit * direction, axis=-1, keepdims=True)) * inverse


def negative_coeffs(scale, offset, a, b):
    return (scale * jax.nn.sigmoid(scale * times_transposed(a, b) + offset)).astype(BF16)


def own_coeffs(scale, offset, a, b):
    scores = scale * times_transposed(a, b) + offset
    rows = lax.broadcasted_iota(jnp.int32, scores.shape, 0)
    columns = lax.broadcasted_iota(jnp.int32, scores.shape, 1)
    label = jnp.where(rows == columns, F32(1.0), F32(-1.0))
    return (-label * scale * jax.nn.sigmoid(-label * scores)).astype(BF16)


def normalize_kernel(values_ref, low_ref):
    values = values_ref[...]
    low_ref[...] = (values * inverse_norm(values)).astype(BF16)


def far_text_kernel(scale_ref, offset_ref, far_ref, own_ref, left_ref, right_ref, out_ref):
    scale, offset = scale_ref[0], offset_ref[0]
    far = far_ref[...]
    total = jnp.zeros(out_ref.shape, F32)
    for image_ref in (own_ref, left_ref, right_ref):
        image = image_ref[...]
        total += times(negative_coeffs(scale, offset, far, image), image)
    out_ref[...] = total.astype(BF16)


def near_kernel(
    scale_ref, offset_ref, image_ref, text_ref, left_image_ref, right_image_ref, left_text_ref, right_text_ref,
    image_dir_ref, text_dir_ref,
):
    scale, offset = scale_ref[0], offset_ref[0]
    image, text = image_ref[...], text_ref[...]
    image_dir = times(own_coeffs(scale, offset, image, text), text)
    text_dir = times(own_coeffs(scale, offset, text, image), image)
    for other_ref in (left_text_ref, right_text_ref):
        other = other_ref[...]
        image_dir += times(negative_coeffs(scale, offset, image, other), other)
    for other_ref in (left_image_ref, right_image_ref):
        other = other_ref[...]
        text_dir += times(negative_coeffs(scale, offset, text, other), other)
    image_dir_ref[...] = image_dir
    text_dir_ref[...] = text_dir


def image_kernel(
    scale_ref, offset_ref, image_ref, near_dir_ref, values_ref, far_ref, far_left_ref, far_right_ref, out_ref
):
    scale, offset = scale_ref[0], offset_ref[0]
    image = image_ref[...]
    direction = near_dir_ref[...]
    for text_ref in (far_ref, far_left_ref, far_right_ref):
        text = text_ref[...]
        direction += times(negative_coeffs(scale, offset, image, text), text)
    out_ref[...] = backward_norm(values_ref[...], direction)


def text_kernel(near_dir_ref, values_ref, far_dir_ref, out_ref):
    direction = near_dir_ref[...] + far_dir_ref[...].astype(F32)
    out_ref[...] = backward_norm(values_ref[...], direction)


def call(body, outs, operands, dots):
    rows, width = operands[-1].shape
    single = not isinstance(outs, tuple)
    shapes = [jax.ShapeDtypeStruct((rows, width), kind) for kind in ((outs,) if single else outs)]
    result = pl.pallas_call(
        body,
        out_shape=shapes[0] if single else tuple(shapes),
        in_specs=[SMEM if o.ndim == 1 else VMEM for o in operands],
        out_specs=VMEM if single else tuple(VMEM for _ in shapes),
        cost_estimate=pl.CostEstimate(
            flops=2 * rows * rows * width * dots,
            bytes_accessed=sum(o.size * o.dtype.itemsize for o in operands) + sum(4 * rows * width for _ in shapes),
            transcendentals=rows * rows * dots,
        ),
    )(*operands)
    return result


def shards(picture_encoder_embeds, caption_encoder_embeds, score_multiplier, score_offset_term):
    groups, halves = lax.axis_size("dp"), lax.axis_size("sub")
    chain = [group * halves + half for half in range(halves) for group in range(groups)]
    onward = [(chain[i], chain[(i + 1) % len(chain)]) for i in range(len(chain))]
    back = [(target, source) for source, target in onward]
    swap = [(0, 1), (1, 0)]
    to_right = lambda block: lax.ppermute(block, ("dp", "sub"), onward)
    to_left = lambda block: lax.ppermute(block, ("dp", "sub"), back)
    across = lambda block: lax.ppermute(block, "sub", swap)

    scalars = (score_multiplier.reshape(1), score_offset_term.reshape(1))
    text = call(normalize_kernel, BF16, (caption_encoder_embeds,), 0)
    image = call(normalize_kernel, BF16, (picture_encoder_embeds,), 0)
    far_text = across(text)
    left_image, right_image = to_right(image), to_left(image)
    left_text, right_text = to_right(text), to_left(text)
    far_left_text, far_right_text = to_right(far_text), to_left(far_text)
    far_dir = across(call(far_text_kernel, BF16, (*scalars, far_text, image, left_image, right_image), 6))
    image_dir, text_dir = call(
        near_kernel, (F32, F32), (*scalars, image, text, left_image, right_image, left_text, right_text), 12
    )
    image_grad = call(
        image_kernel,
        F32,
        (*scalars, image, image_dir, picture_encoder_embeds, far_text, far_left_text, far_right_text),
        6,
    )
    text_grad = call(text_kernel, F32, (text_dir, caption_encoder_embeds, far_dir), 0)
    return (image_grad, text_grad)


def solution(mesh):
    placed = (P(("dp", "sub"), None), P(("dp", "sub"), None), P(), P())
    return jax.shard_map(
        shards,
        mesh=mesh,
        in_specs=placed,
        out_specs=(P(("dp", "sub"), None), P(("dp", "sub"), None)),
        check_vma=False,
    )
```

```python
import jax
import jax.numpy as jnp
from jax import lax
from jax.sharding import PartitionSpec as P

BF16 = jnp.bfloat16
F32 = jnp.float32


def times_transposed(a, b):
    return lax.dot_general(a, b, (((1,), (1,)), ((), ())), preferred_element_type=F32)


def times(a, b):
    return lax.dot_general(a, b, (((1,), (0,)), ((), ())), preferred_element_type=F32)


def normalize(values):
    inverse = lax.rsqrt(jnp.sum(values * values, axis=-1, keepdims=True) + 1e-06)
    return (values * inverse).astype(BF16), inverse


def backward_norm(values, inverse, direction):
    unit = values * inverse
    return (direction - unit * jnp.sum(unit * direction, axis=-1, keepdims=True)) * inverse


def transposed_times(a, b):
    return lax.dot_general(a, b, (((0,), (0,)), ((), ())), preferred_element_type=F32)


def band_coeffs(scale, offset, images, texts, rows):
    scores = scale * times_transposed(images, texts) + offset
    image_ids = lax.broadcasted_iota(jnp.int32, scores.shape, 0)
    text_ids = lax.broadcasted_iota(jnp.int32, scores.shape, 1)
    label = jnp.where((image_ids == text_ids) & (image_ids < rows), F32(1.0), F32(-1.0))
    coeffs = (-label * scale * jax.nn.sigmoid(-label * scores)).astype(BF16)
    return lax.optimization_barrier(coeffs)


def shards(picture_encoder_embeds, caption_encoder_embeds, score_multiplier, score_offset_term):
    groups, halves = lax.axis_size("dp"), lax.axis_size("sub")
    chain = [group * halves + half for half in range(halves) for group in range(groups)]
    onward = [(chain[i], chain[(i + 1) % len(chain)]) for i in range(len(chain))]
    back = [(target, source) for source, target in onward]
    swap = [(0, 1), (1, 0)]
    to_right = lambda block: lax.ppermute(block, ("dp", "sub"), onward)
    to_left = lambda block: lax.ppermute(block, ("dp", "sub"), back)
    across = lambda block: lax.ppermute(block, "sub", swap)
    rows = picture_encoder_embeds.shape[0]
    after = lambda value, earlier: lax.optimization_barrier((value, earlier))[0]

    text, text_inverse = normalize(caption_encoder_embeds)
    far_text = across(text)
    image, image_inverse = normalize(after(picture_encoder_embeds, text))
    left_image, right_image = to_right(image), to_left(image)
    texts = jnp.concatenate([text, far_text])
    own = band_coeffs(score_multiplier, score_offset_term, image, texts, rows)
    left_image, right_image, own = lax.optimization_barrier((left_image, right_image, own))
    sides = jnp.concatenate([left_image, right_image])
    side_coeffs = band_coeffs(score_multiplier, score_offset_term, sides, texts, 0)
    images = jnp.concatenate([image, sides])
    coeffs = jnp.concatenate([own, side_coeffs])
    far_dir = transposed_times(coeffs[:, rows:], images).astype(BF16)
    coeffs, far_dir = lax.optimization_barrier((coeffs, far_dir))
    far_dir = across(far_dir)
    right_dir = times(coeffs[2 * rows :], texts).astype(BF16)
    from_left = to_right(right_dir)
    left_dir = times(coeffs[rows : 2 * rows], texts).astype(BF16)
    from_right = to_left(left_dir)
    text_dir = transposed_times(coeffs[:, :rows], images) + far_dir.astype(F32)
    text_grad = backward_norm(caption_encoder_embeds, text_inverse, text_dir)
    from_left, from_right, text_grad = lax.optimization_barrier((from_left, from_right, text_grad))
    image_dir = times(coeffs[:rows], texts) + from_left.astype(F32) + from_right.astype(F32)
    image_grad = backward_norm(picture_encoder_embeds, image_inverse, image_dir)
    return (image_grad, text_grad)


def solution(mesh):
    placed = (P(("dp", "sub"), None), P(("dp", "sub"), None), P(), P())
    return jax.shard_map(
        shards,
        mesh=mesh,
        in_specs=placed,
        out_specs=(P(("dp", "sub"), None), P(("dp", "sub"), None)),
        check_vma=False,
    )
```

```python
import jax
import jax.numpy as jnp
from jax import lax
from jax.sharding import PartitionSpec as P

BF16 = jnp.bfloat16
F32 = jnp.float32


def times_transposed(a, b):
    return lax.dot_general(a, b, (((1,), (1,)), ((), ())), preferred_element_type=F32)


def times(a, b):
    return lax.dot_general(a, b, (((1,), (0,)), ((), ())), preferred_element_type=F32)


def normalize(values):
    inverse = lax.rsqrt(jnp.sum(values * values, axis=-1, keepdims=True) + 1e-06)
    return (values * inverse).astype(BF16), inverse


def backward_norm(values, inverse, direction):
    unit = values * inverse
    return (direction - unit * jnp.sum(unit * direction, axis=-1, keepdims=True)) * inverse


def transposed_times(a, b):
    return lax.dot_general(a, b, (((0,), (0,)), ((), ())), preferred_element_type=F32)


def band_coeffs(scale, offset, images, texts, rows):
    scores = scale * times_transposed(images, texts) + offset
    image_ids = lax.broadcasted_iota(jnp.int32, scores.shape, 0)
    text_ids = lax.broadcasted_iota(jnp.int32, scores.shape, 1)
    label = jnp.where((image_ids == text_ids) & (image_ids < rows), F32(1.0), F32(-1.0))
    coeffs = (-label * scale * jax.nn.sigmoid(-label * scores)).astype(BF16)
    return lax.optimization_barrier(coeffs)


def shards(picture_encoder_embeds, caption_encoder_embeds, score_multiplier, score_offset_term):
    groups, halves = lax.axis_size("dp"), lax.axis_size("sub")
    chain = [group * halves + half for half in range(halves) for group in range(groups)]
    onward = [(chain[i], chain[(i + 1) % len(chain)]) for i in range(len(chain))]
    back = [(target, source) for source, target in onward]
    swap = [(0, 1), (1, 0)]
    to_right = lambda block: lax.ppermute(block, ("dp", "sub"), onward)
    to_left = lambda block: lax.ppermute(block, ("dp", "sub"), back)
    across = lambda block: lax.ppermute(block, "sub", swap)
    rows = picture_encoder_embeds.shape[0]
    after = lambda value, earlier: lax.optimization_barrier((value, earlier))[0]

    text, text_inverse = normalize(caption_encoder_embeds)
    far_text = across(text)
    image, image_inverse = normalize(after(picture_encoder_embeds, text))
    right_image, left_image = to_left(image), to_right(image)
    texts = jnp.concatenate([text, far_text])
    own = band_coeffs(score_multiplier, score_offset_term, image, texts, rows)
    right_image, left_image, own = lax.optimization_barrier((right_image, left_image, own))
    sides = jnp.concatenate([left_image, right_image])
    side_coeffs = band_coeffs(score_multiplier, score_offset_term, sides, texts, 0)
    images = jnp.concatenate([image, sides])
    coeffs = jnp.concatenate([own, side_coeffs])
    right_dir = times(coeffs[2 * rows :], texts).astype(BF16)
    from_left = to_right(right_dir)
    far_coeffs = after(coeffs[:, rows:], right_dir)
    far_dir = transposed_times(far_coeffs, images).astype(BF16)
    left_coeffs = after(coeffs[rows : 2 * rows], far_dir)
    far_dir = across(far_dir)
    left_dir = times(left_coeffs, texts).astype(BF16)
    from_right = to_left(left_dir)
    image_part = times(coeffs[:rows], texts) + from_left.astype(F32)
    far_dir, image_part = lax.optimization_barrier((far_dir, image_part))
    text_dir = transposed_times(coeffs[:, :rows], images) + far_dir.astype(F32)
    text_grad = backward_norm(caption_encoder_embeds, text_inverse, text_dir)
    from_right, text_grad = lax.optimization_barrier((from_right, text_grad))
    image_dir = image_part + from_right.astype(F32)
    image_grad = backward_norm(picture_encoder_embeds, image_inverse, image_dir)
    return (image_grad, text_grad)


def solution(mesh):
    placed = (P(("dp", "sub"), None), P(("dp", "sub"), None), P(), P())
    return jax.shard_map(
        shards,
        mesh=mesh,
        in_specs=placed,
        out_specs=(P(("dp", "sub"), None), P(("dp", "sub"), None)),
        check_vma=False,
    )
```

```python
import jax
import jax.numpy as jnp
from jax import lax
from jax.sharding import PartitionSpec as P

BF16 = jnp.bfloat16
F32 = jnp.float32


def times_transposed(a, b):
    return lax.dot_general(a, b, (((1,), (1,)), ((), ())), preferred_element_type=F32)


def times(a, b):
    return lax.dot_general(a, b, (((1,), (0,)), ((), ())), preferred_element_type=F32)


def normalize(values):
    inverse = lax.rsqrt(jnp.sum(values * values, axis=-1, keepdims=True) + 1e-06)
    return (values * inverse).astype(BF16), inverse


def backward_norm(values, inverse, direction):
    unit = values * inverse
    return (direction - unit * jnp.sum(unit * direction, axis=-1, keepdims=True)) * inverse


def transposed_times(a, b):
    return lax.dot_general(a, b, (((0,), (0,)), ((), ())), preferred_element_type=F32)


def band_coeffs(scale, offset, images, texts, rows):
    scores = scale * times_transposed(images, texts) + offset
    image_ids = lax.broadcasted_iota(jnp.int32, scores.shape, 0)
    text_ids = lax.broadcasted_iota(jnp.int32, scores.shape, 1)
    label = jnp.where((image_ids == text_ids) & (image_ids < rows), F32(1.0), F32(-1.0))
    coeffs = (-label * scale * jax.nn.sigmoid(-label * scores)).astype(BF16)
    return lax.optimization_barrier(coeffs)


def shards(picture_encoder_embeds, caption_encoder_embeds, score_multiplier, score_offset_term):
    groups, halves = lax.axis_size("dp"), lax.axis_size("sub")
    chain = [group * halves + half for half in range(halves) for group in range(groups)]
    onward = [(chain[i], chain[(i + 1) % len(chain)]) for i in range(len(chain))]
    back = [(target, source) for source, target in onward]
    swap = [(group * halves + half, group * halves + 1 - half) for group in range(groups) for half in range(halves)]
    late = [pair for pair in swap if pair[0] // halves % 16 == 15]
    early = [pair for pair in swap if pair[0] // halves % 16 != 15]
    send = lambda block, pairs: lax.ppermute(block, ("dp", "sub"), pairs)
    rows = picture_encoder_embeds.shape[0]
    after = lambda value, earlier: lax.optimization_barrier((value, earlier))[0]

    text, text_inverse = normalize(caption_encoder_embeds)
    far_text = send(text, swap)
    image, image_inverse = normalize(after(picture_encoder_embeds, text))
    right_image, left_image = send(image, back), send(image, onward)
    texts = jnp.concatenate([text, far_text])
    own = band_coeffs(score_multiplier, score_offset_term, image, texts, rows)
    left_image, right_image, own = lax.optimization_barrier((left_image, right_image, own))
    sides = jnp.concatenate([left_image, right_image])
    side_coeffs = band_coeffs(score_multiplier, score_offset_term, sides, texts, 0)
    images = jnp.concatenate([image, sides])
    coeffs = jnp.concatenate([own, side_coeffs])
    place = lax.axis_index("dp") % 16
    far_dir = transposed_times(coeffs[:, rows:], images).astype(BF16)
    right_dir = times(after(coeffs[2 * rows :], far_dir), texts).astype(BF16)
    early_dir = send(far_dir, early)
    from_left = send(right_dir, onward)
    left_dir = times(after(coeffs[rows : 2 * rows], right_dir), texts).astype(BF16)
    from_right = send(left_dir, back)
    late_block = jnp.where(place == 15, after(far_dir, left_dir), jnp.zeros_like(far_dir))
    late_dir = send(late_block, late)
    text_part = transposed_times(coeffs[:, :rows], images) + early_dir.astype(F32)
    from_left, text_part = lax.optimization_barrier((from_left, text_part))
    image_part = times(coeffs[:rows], texts) + from_left.astype(F32)
    late_dir, image_part = lax.optimization_barrier((late_dir, image_part))
    text_dir = text_part + late_dir.astype(F32)
    text_grad = backward_norm(caption_encoder_embeds, text_inverse, text_dir)
    from_right, text_grad = lax.optimization_barrier((from_right, text_grad))
    image_dir = image_part + from_right.astype(F32)
    image_grad = backward_norm(picture_encoder_embeds, image_inverse, image_dir)
    return (image_grad, text_grad)


def solution(mesh):
    placed = (P(("dp", "sub"), None), P(("dp", "sub"), None), P(), P())
    return jax.shard_map(
        shards,
        mesh=mesh,
        in_specs=placed,
        out_specs=(P(("dp", "sub"), None), P(("dp", "sub"), None)),
        check_vma=False,
    )
```

```python
import jax
import jax.numpy as jnp
from jax import lax
from jax.sharding import PartitionSpec as P

BF16 = jnp.bfloat16
F32 = jnp.float32


def times_transposed(a, b):
    return lax.dot_general(a, b, (((1,), (1,)), ((), ())), preferred_element_type=F32)


def times(a, b):
    return lax.dot_general(a, b, (((1,), (0,)), ((), ())), preferred_element_type=F32)


def normalize(values):
    inverse = lax.rsqrt(jnp.sum(values * values, axis=-1, keepdims=True) + 1e-06)
    return (values * inverse).astype(BF16), inverse


def backward_norm(values, inverse, direction):
    unit = values * inverse
    return (direction - unit * jnp.sum(unit * direction, axis=-1, keepdims=True)) * inverse


def transposed_times(a, b):
    return lax.dot_general(a, b, (((0,), (0,)), ((), ())), preferred_element_type=F32)


def band_coeffs(scale, offset, images, texts, rows):
    scores = scale * times_transposed(images, texts) + offset
    image_ids = lax.broadcasted_iota(jnp.int32, scores.shape, 0)
    text_ids = lax.broadcasted_iota(jnp.int32, scores.shape, 1)
    label = jnp.where((image_ids == text_ids) & (image_ids < rows), F32(1.0), F32(-1.0))
    coeffs = (-label * scale * jax.nn.sigmoid(-label * scores)).astype(BF16)
    return lax.optimization_barrier(coeffs)


def shards(picture_encoder_embeds, caption_encoder_embeds, score_multiplier, score_offset_term):
    groups, halves = lax.axis_size("dp"), lax.axis_size("sub")
    chain = [group * halves + half for half in range(halves) for group in range(groups)]
    onward = [(chain[i], chain[(i + 1) % len(chain)]) for i in range(len(chain))]
    back = [(target, source) for source, target in onward]
    swap = [(group * halves + half, group * halves + 1 - half) for group in range(groups) for half in range(halves)]
    late = [pair for pair in swap if pair[0] // halves % 16 == 15]
    early = [pair for pair in swap if pair[0] // halves % 16 != 15]
    wraps, inner = onward[127::128], [pair for i, pair in enumerate(onward) if i % 128 != 127]
    send = lambda block, pairs: lax.ppermute(block, ("dp", "sub"), pairs)
    rows = picture_encoder_embeds.shape[0]
    after = lambda value, earlier: lax.optimization_barrier((value, earlier))[0]

    text, text_inverse = normalize(caption_encoder_embeds)
    far_text = send(text, swap)
    image, image_inverse = normalize(after(picture_encoder_embeds, text))
    right_image, left_image = send(image, back), send(image, onward)
    texts = jnp.concatenate([text, far_text])
    own = band_coeffs(score_multiplier, score_offset_term, image, texts, rows)
    left_image, right_image, own = lax.optimization_barrier((left_image, right_image, own))
    sides = jnp.concatenate([left_image, right_image])
    side_coeffs = band_coeffs(score_multiplier, score_offset_term, sides, texts, 0)
    images = jnp.concatenate([image, sides])
    coeffs = jnp.concatenate([own, side_coeffs])
    place = lax.axis_index("dp") % 16
    right_dir = times(coeffs[2 * rows :], texts).astype(BF16)
    far_dir = transposed_times(after(coeffs[:, rows:], right_dir), images).astype(BF16)
    from_wrap = send(right_dir, wraps)
    early_dir = send(far_dir, early)
    right_dir = jnp.where(place < 16, after(right_dir, far_dir), jnp.zeros_like(right_dir))
    from_left = send(right_dir, inner)
    left_dir = times(after(coeffs[rows : 2 * rows], right_dir), texts).astype(BF16)
    from_right = send(left_dir, back)
    late_block = jnp.where(place == 15, after(far_dir, left_dir), jnp.zeros_like(far_dir))
    late_dir = send(late_block, late)
    image_part = times(coeffs[:rows], texts) + from_wrap.astype(F32) + from_left.astype(F32)
    from_right, image_part = lax.optimization_barrier((from_right, image_part))
    image_dir = image_part + from_right.astype(F32)
    image_grad = backward_norm(picture_encoder_embeds, image_inverse, image_dir)
    early_dir, image_grad = lax.optimization_barrier((early_dir, image_grad))
    text_part = transposed_times(coeffs[:, :rows], images) + early_dir.astype(F32)
    late_dir, text_part = lax.optimization_barrier((late_dir, text_part))
    text_dir = text_part + late_dir.astype(F32)
    text_grad = backward_norm(caption_encoder_embeds, text_inverse, text_dir)
    return (image_grad, text_grad)


def solution(mesh):
    placed = (P(("dp", "sub"), None), P(("dp", "sub"), None), P(), P())
    return jax.shard_map(
        shards,
        mesh=mesh,
        in_specs=placed,
        out_specs=(P(("dp", "sub"), None), P(("dp", "sub"), None)),
        check_vma=False,
    )
```
